32 devices in a mesh: seq: 16 (over z, y, core), width: 2 (over x).
Axes of the slice: x: 2, y: 2, z: 4, core: 2. Of those that a mesh axis runs over, the one named last changes fastest.
Arguments:
- tokens: bfloat16 [16384, 16384], P('seq', 'width'), may hold values from -6 to 6
- panel_weights: bfloat16 [2, 16384, 1024], P(None, 'width', 'seq'), may hold values from -0.046875 to 0.046875
- panel_scales: float32 [2, 1024, 1024], P(None, 'width', 'seq'), may hold values from 0.4 to 2.5
- doc_lengths: int32 [16, 8], P('seq'), may hold values from 0 to 1024, as said below
Outputs:
- hidden: float32 [16384, 1024], P(('seq', 'width'))
The draws below stay inside these ranges and needn't reach their ends.
Inputs may be any that keep to these rules, and one draw needn't show every extreme that they name: `doc_lengths`: each row sums to at most 1024; some row holds one document of exactly 1024; documents may be empty.
All inputs are finite; a program needn't handle non-finite values.
Results may differ from the reference program's by a relative error of at most 0.014.
Values may be sent and summed in bfloat16 or wider, within the bound.
A program may use at most 128 MiB of HBM per device.

```python
import math
import jax
import jax.numpy as jnp

D = 16384
PANEL = 1024
DOCS = 8
TOK_DEV = 1024
TOKENS = 16384
N_SEQ = 16


def draw_doc_lengths(key, part):
    first, second, third = jax.random.split(jax.random.fold_in(key, 7), 3)
    filled = jax.random.randint(first, (N_SEQ,), TOK_DEV // 8, TOK_DEV // 2 + 1)
    busiest = jax.random.randint(second, (), 0, N_SEQ)
    filled = jnp.where(jnp.arange(N_SEQ) == busiest, TOK_DEV, filled).astype(jnp.int32)
    cut_points = jax.random.randint(third, (N_SEQ, DOCS - 1), 0, TOK_DEV + 1)
    cut_points = jnp.sort(jnp.minimum(cut_points, filled[:, None]), axis=1).astype(jnp.int32)
    edges = jnp.concatenate([jnp.zeros((N_SEQ, 1), jnp.int32), cut_points, filled[:, None]], axis=1)
    lengths = jnp.diff(edges, axis=1).astype(jnp.int32)
    single = jnp.where(jnp.arange(DOCS)[None, :] == 0, TOK_DEV, 0).astype(jnp.int32)
    return jnp.where(jnp.arange(N_SEQ)[:, None] == busiest, single, lengths).astype(jnp.int32)


def levels(stream_key, dims, cuts, smallest, top_value):
    gain, own = 1.0, jax.random.fold_in(stream_key, 6)
    for axis_at, parts in cuts:
        heights = jnp.exp(jax.random.uniform(jax.random.fold_in(own, axis_at), (parts,), jnp.float32, smallest / len(cuts), top_value / len(cuts)))
        gain = gain * jnp.repeat(heights, dims[axis_at] // parts).reshape([-1 if axis == axis_at else 1 for axis in range(len(dims))])
    return gain


def bell_draw(key, shape, deviation, limit, cuts=(), kind=jnp.bfloat16):
    gain = levels(key, shape, cuts, -0.22, 0.18) if cuts else 1.0
    entries = jax.random.normal(key, shape, jnp.float32) * deviation * gain
    return jnp.minimum(jnp.maximum(entries, -limit), limit).astype(kind)


def setup_inputs(seed: int = 0) -> dict:
    keys = jax.random.split(jax.random.key(seed), 5)
    tokens = bell_draw(keys[0], (TOKENS, D), 1.0, 6.0, ((0, 16), (1, 2)))
    panel_weights = bell_draw(keys[1], (2, D, PANEL), D ** -0.5, 0.046875, ((1, 2), (2, 16)))
    panel_scales = jnp.clip(jnp.exp(math.log(2.5) - 1.8325814 * jax.random.uniform(keys[2], (2, D // 16, PANEL), jnp.float32) ** levels(keys[2], (2, D // 16, PANEL), ((1, 2), (2, 16)), -0.2, 0.2)), 0.4, 2.5)
    doc_lengths = draw_doc_lengths(jax.random.fold_in(keys[4], 71), 0)
    return dict(tokens=tokens, panel_weights=panel_weights, panel_scales=panel_scales, doc_lengths=doc_lengths)


def dequantize(weights, scales):
    spread = jnp.repeat(scales, 16, axis=1)
    return (weights.astype(jnp.float32) * spread).astype(jnp.bfloat16)


def reference(tokens, panel_weights, panel_scales, doc_lengths):
    weights_deq = dequantize(panel_weights, panel_scales)
    gate = jnp.dot(tokens, weights_deq[0], preferred_element_type=jnp.float32)
    upward = jnp.dot(tokens, weights_deq[1], preferred_element_type=jnp.float32)
    mixed = jax.nn.silu(gate) * upward
    live_count = jnp.sum(doc_lengths, axis=1).astype(jnp.int32)
    index_all = jnp.arange(TOKENS, dtype=jnp.int32)
    owner = index_all // TOK_DEV
    position = index_all % TOK_DEV
    keep = position < live_count[owner]
    return jnp.where(keep[:, None], mixed, jnp.float32(0.0)).astype(jnp.float32)
```

```python
import functools

import jax
import jax.numpy as jnp
from jax import lax
from jax.experimental import pallas as pl
from jax.experimental.pallas import tpu as pltpu
from jax.sharding import PartitionSpec as P

MESH = pl.DeviceIdType.MESH
GROUP = 16
LEFT, RIGHT, ACROSS, SIBLING = range(4)


def pick(values, at):
    found = jnp.int32(values[0])
    for k in range(1, len(values)):
        found = jnp.where(at == k, jnp.int32(values[k]), found)
    return found


def kernel(
    n_seq, n_width, pieces,
    weights, scales, tokens, out,
    gathered, tok, spread_mat, acc, keep_up, send_buf, recv_buf,
    send_sem, recv_sem, x_send, x_recv, w_sem, tok_sem,
):
    n_z = n_seq // 4
    me, wid = lax.axis_index("seq"), lax.axis_index("width")
    core, chip = lax.rem(me, 2), me // 2
    y, z = lax.rem(chip, 2), chip // 2
    far = 1 - y
    rows, depth = weights.shape[1], weights.shape[2]
    per_half = pieces // 2
    r_piece = rows // per_half
    n_tok = tokens.shape[0]
    share = n_tok // n_width
    n_cols = 4 * rows

    def seq_of(zz, yy, cc):
        return {"seq": (zz * 2 + yy) * 2 + cc}

    target = {
        LEFT: seq_of(lax.rem(z + n_z - 1, n_z), y, core),
        RIGHT: seq_of(lax.rem(z + 1, n_z), y, core),
        ACROSS: seq_of(z, far, core),
        SIBLING: seq_of(z, y, 1 - core),
    }

    def block(c, p, half):
        return gathered.at[c, p // per_half, half, pl.ds((p % per_half) * r_piece, r_piece), :]

    def copy(c, p, way):
        return pltpu.make_async_remote_copy(
            src_ref=block(c, p, core), dst_ref=block(c, p, core),
            send_sem=send_sem.at[way, c, p], recv_sem=recv_sem.at[core, c, p],
            device_id=target[way], device_id_type=MESH,
        )

    def arrived(c, p, half):
        pltpu.make_async_remote_copy(
            src_ref=block(c, p, half), dst_ref=block(c, p, half),
            send_sem=send_sem.at[SIBLING, c, p], recv_sem=recv_sem.at[half, c, p],
            device_id=target[SIBLING], device_id_type=MESH,
        ).wait_recv()

    def x_copy(d, c):
        return pltpu.make_async_remote_copy(
            src_ref=send_buf.at[d - 1, c], dst_ref=recv_buf.at[d - 1, c],
            send_sem=x_send.at[d - 1, c], recv_sem=x_recv.at[d - 1, c],
            device_id={"width": lax.rem(wid + d, n_width)}, device_id_type=MESH,
        )

    w_copies = [
        pltpu.make_async_copy(weights.at[g], gathered.at[chip, g, core], w_sem.at[g])
        for g in range(2)
    ]
    for c in w_copies:
        c.start()
    tok_copy = pltpu.make_async_copy(tokens, tok, tok_sem)
    tok_copy.start()

    barrier = pltpu.get_barrier_semaphore()
    for way in range(4):
        pl.semaphore_signal(barrier, inc=1, device_id=target[way], device_id_type=MESH)
    for d in range(1, n_width):
        pl.semaphore_signal(
            barrier, inc=1, device_id={"width": lax.rem(wid + d, n_width)}, device_id_type=MESH
        )

    chunk = spread_mat.shape[0]
    wide = chunk * GROUP
    at_row = lax.broadcasted_iota(jnp.int32, (chunk, wide), 0)
    at_col = lax.broadcasted_iota(jnp.int32, (chunk, wide), 1)
    first_col = at_row * GROUP
    spread_mat[...] = jnp.where(
        (at_col >= first_col) & (at_col < first_col + GROUP), 1.0, 0.0
    ).astype(jnp.bfloat16)

    pl.semaphore_wait(barrier, 4 + n_width - 1)

    for p in range(pieces):
        g, row = p // per_half, (p % per_half) * r_piece
        if p % per_half == 0:
            w_copies[g].wait()

        @pl.loop(0, scales.shape[2] // chunk)
        def _(j):
            s = scales[g, pl.ds(row, r_piece), pl.ds(pl.multiple_of(j * chunk, chunk), chunk)]
            high = s.astype(jnp.bfloat16)
            rest = s - high.astype(jnp.float32)
            mid = rest.astype(jnp.bfloat16)
            low = (rest - mid.astype(jnp.float32)).astype(jnp.bfloat16)
            parts = jnp.dot(
                jnp.concatenate([high, mid, low], axis=0), spread_mat[...],
                preferred_element_type=jnp.float32,
            )
            spread = parts[:r_piece] + parts[r_piece:2 * r_piece] + parts[2 * r_piece:]
            cols = pl.ds(pl.multiple_of(j * wide, wide), wide)
            w = gathered[chip, g, core, pl.ds(row, r_piece), cols].astype(jnp.float32)
            gathered[chip, g, core, pl.ds(row, r_piece), cols] = (w * spread).astype(jnp.bfloat16)

        @pl.when(z > 0)
        def _():
            copy(chip, p, LEFT).start()

        @pl.when(z < n_z - 1)
        def _():
            copy(chip, p, RIGHT).start()

        copy(chip, p, ACROSS).start()
        copy(chip, p, SIBLING).start()

    tok_copy.wait()

    k_step = min(1024, depth)

    def compute(c):
        for p in range(pieces):
            arrived(c, p, 1 - core)

        def dot(k):
            at = pl.ds(pl.multiple_of(k * k_step, k_step), k_step)
            b = gathered[c, :, :, :, at].reshape(n_cols, k_step)
            return lax.dot_general(
                tok[:, at], b, (((1,), (1,)), ((), ())), preferred_element_type=jnp.float32
            )

        acc[...] = dot(0)

        @pl.loop(1, depth // k_step)
        def _(k):
            acc[...] += dot(k)

        mine = pl.ds(pl.multiple_of(wid * share, share), share)
        half_cols = n_cols // 2
        out[c] = acc[mine, :half_cols]
        keep_up[c] = acc[mine, half_cols:]
        for d in range(1, n_width):
            other = pl.ds(pl.multiple_of(lax.rem(wid + d, n_width) * share, share), share)
            send_buf[d - 1, c] = acc[other, :].astype(jnp.bfloat16)
            x_copy(d, c).start()

    def finish(c):
        half_cols = n_cols // 2
        for d in range(1, n_width):
            x_copy(d, c).wait_recv()
        gate, up = out[c], keep_up[c]
        for d in range(1, n_width):
            both = recv_buf[d - 1, c].astype(jnp.float32)
            gate, up = gate + both[:, :half_cols], up + both[:, half_cols:]
        out[c] = gate / (1.0 + jnp.exp(-gate)) * up

    orders = []
    for zz in range(n_z):
        order = [zz]
        for r in range(1, n_z):
            order += [b for b in (zz - r, zz + r) if 0 <= b < n_z]
        orders.append(order)
    nearest = [pick([orders[zz][k] for zz in range(n_z)], z) for k in range(n_z)]
    half_way = n_z // 2
    lent = jnp.where(z < half_way, z + 1, z - 1)
    lend_left = (z > 0) & (z - 1 < half_way)
    lend_right = (z < n_z - 1) & (z + 1 >= half_way)
    lent_pieces = range(pieces // 2, pieces)

    def over_y(k, p):
        return nearest[k] != lent if p in lent_pieces and k > 0 else z >= 0

    def blocks_of(r):
        found = []
        if 0 < r < n_z:
            found.append((z - r >= 0, (z - r) * 2 + y))
            found.append((z + r < n_z, (z + r) * 2 + y))
        if r > 0:
            whole = nearest[r - 1] != lent if r > 1 else z >= 0
            found.append((whole, nearest[r - 1] * 2 + far))
        else:
            found.append((z >= 0, chip))
        return found

    def guarded(f, cond, c):
        @pl.when(cond)
        def _():
            f(c)

    for r in range(1, n_z + 1):
        for p in range(pieces):
            if r < n_z:
                from_left, from_right = (z - r) * 2 + y, (z + r) * 2 + y

                @pl.when(z - r >= 0)
                def _():
                    arrived(from_left, p, core)

                    @pl.when(z < n_z - 1)
                    def _():
                        copy(from_left, p, RIGHT).start()

                    copy(from_left, p, SIBLING).start()

                @pl.when(z + r < n_z)
                def _():
                    arrived(from_right, p, core)

                    @pl.when(z > 0)
                    def _():
                        copy(from_right, p, LEFT).start()

                    copy(from_right, p, SIBLING).start()

                @pl.when(over_y(r, p))
                def _():
                    copy(nearest[r] * 2 + y, p, ACROSS).start()

            @pl.when(over_y(r - 1, p))
            def _():
                c = nearest[r - 1] * 2 + far
                arrived(c, p, core)
                copy(c, p, SIBLING).start()

            ready = blocks_of(r - 1)
            if p < len(ready):
                guarded(compute, *ready[p])
            if r > 1 and p == pieces - 1:
                for cond, c in blocks_of(r - 2):
                    guarded(finish, cond, c)

        if r == n_z - 1:
            own_far = z * 2 + far
            for p in lent_pieces:
                @pl.when(lend_left)
                def _():
                    copy(own_far, p, LEFT).start()

                @pl.when(lend_right)
                def _():
                    copy(own_far, p, RIGHT).start()

    lent_chip = lent * 2 + far
    for p in lent_pieces:
        arrived(lent_chip, p, core)
        copy(lent_chip, p, SIBLING).start()
    for cond, c in blocks_of(n_z - 1):
        guarded(finish, cond, c)
    last = blocks_of(n_z)
    for cond, c in last:
        guarded(compute, cond, c)
    compute(lent_chip)
    for cond, c in last:
        guarded(finish, cond, c)
    finish(lent_chip)

    for zz in range(n_z):
        for p in range(pieces):
            own, other = zz * 2 + y, zz * 2 + far

            @pl.when((z > 0) & (z <= zz))
            def _():
                copy(own, p, LEFT).wait_send()

            @pl.when((z < n_z - 1) & (z >= zz))
            def _():
                copy(own, p, RIGHT).wait_send()

            if p in lent_pieces:
                @pl.when((zz == z) & lend_left)
                def _():
                    copy(other, p, LEFT).wait_send()

                @pl.when((zz == z) & lend_right)
                def _():
                    copy(other, p, RIGHT).wait_send()

                @pl.when(zz != lent)
                def _():
                    copy(own, p, ACROSS).wait_send()
            else:
                copy(own, p, ACROSS).wait_send()
            copy(own, p, SIBLING).wait_send()
            copy(other, p, SIBLING).wait_send()
    for c in range(n_z * 2):
        for d in range(1, n_width):
            x_copy(d, c).wait_send()


def per_device(tokens, panel_weights, panel_scales, doc_lengths):
    n_seq, n_width = lax.axis_size("seq"), lax.axis_size("width")
    n_tok, depth = tokens.shape
    cols = panel_weights.shape[2]
    share = n_tok // n_width
    chips = n_seq // 2
    pieces = 4
    chunk = min(128, panel_scales.shape[1])
    bf16, f32 = jnp.bfloat16, jnp.float32
    blocks = pl.pallas_call(
        functools.partial(kernel, n_seq, n_width, pieces),
        out_shape=jax.ShapeDtypeStruct((chips, share, 2 * cols), f32),
        in_specs=[
            pl.BlockSpec(memory_space=pl.ANY),
            pl.BlockSpec(memory_space=pltpu.VMEM),
            pl.BlockSpec(memory_space=pl.ANY),
        ],
        out_specs=pl.BlockSpec(memory_space=pltpu.VMEM),
        scratch_shapes=[
            pltpu.VMEM((chips, 2, 2, cols, depth), bf16),
            pltpu.VMEM((n_tok, depth), bf16),
            pltpu.VMEM((chunk, chunk * GROUP), bf16),
            pltpu.VMEM((n_tok, 4 * cols), f32),
            pltpu.VMEM((chips, share, 2 * cols), f32),
            pltpu.VMEM((max(n_width - 1, 1), chips, share, 4 * cols), bf16),
            pltpu.VMEM((max(n_width - 1, 1), chips, share, 4 * cols), bf16),
            pltpu.SemaphoreType.DMA((4, chips, pieces)),
            pltpu.SemaphoreType.DMA((2, chips, pieces)),
            pltpu.SemaphoreType.DMA((max(n_width - 1, 1), chips)),
            pltpu.SemaphoreType.DMA((max(n_width - 1, 1), chips)),
            pltpu.SemaphoreType.DMA((2,)),
            pltpu.SemaphoreType.DMA,
        ],
        compiler_params=pltpu.CompilerParams(
            collective_id=0, has_side_effects=True, vmem_limit_bytes=62 * 1024 * 1024
        ),
        cost_estimate=pl.CostEstimate(
            flops=2 * n_tok * depth * 2 * cols * n_seq,
            bytes_accessed=2 * n_tok * depth + 4 * cols * depth,
            transcendentals=share * cols * n_seq,
        ),
    )(jnp.swapaxes(panel_weights, 1, 2), jnp.swapaxes(panel_scales, 1, 2), tokens)
    mixed = jnp.transpose(blocks, (1, 0, 2)).reshape(share, cols * n_seq)
    position = lax.axis_index("width") * share + jnp.arange(share, dtype=jnp.int32)
    keep = position < jnp.sum(doc_lengths)
    return jnp.where(keep[:, None], mixed, jnp.zeros_like(mixed))


def solution(mesh):
    in_specs = (P("seq", "width"), P(None, "width", "seq"), P(None, "width", "seq"), P("seq", None))
    out_specs = P(("seq", "width"), None)
    return jax.shard_map(
        per_device, mesh=mesh, in_specs=in_specs, out_specs=out_specs, check_vma=False
    )
```

```python
import functools

import jax
import jax.numpy as jnp
from jax import lax
from jax.experimental import pallas as pl
from jax.experimental.pallas import tpu as pltpu
from jax.sharding import PartitionSpec as P

MESH = pl.DeviceIdType.MESH
GROUP = 16
LEFT, RIGHT, ACROSS, SIBLING = range(4)


def pick(values, at):
    found = jnp.int32(values[0])
    for k in range(1, len(values)):
        found = jnp.where(at == k, jnp.int32(values[k]), found)
    return found


def kernel(
    n_seq, n_width, pieces,
    weights, scales, tokens, doc_lengths, out,
    gathered, tok, spread_mat, acc, kept, send_buf, recv_buf,
    send_sem, recv_sem, x_send, x_recv, w_sem, tok_sem,
):
    n_z = n_seq // 4
    me, wid = lax.axis_index("seq"), lax.axis_index("width")
    core, chip = lax.rem(me, 2), me // 2
    y, z = lax.rem(chip, 2), chip // 2
    far = 1 - y
    rows, depth = weights.shape[1], weights.shape[2]
    per_half = pieces // 2
    r_piece = rows // per_half
    n_tok = tokens.shape[0]
    share = n_tok // n_width
    n_cols = 4 * rows

    def seq_of(zz, yy, cc):
        return {"seq": (zz * 2 + yy) * 2 + cc}

    target = {
        LEFT: seq_of(lax.rem(z + n_z - 1, n_z), y, core),
        RIGHT: seq_of(lax.rem(z + 1, n_z), y, core),
        ACROSS: seq_of(z, far, core),
        SIBLING: seq_of(z, y, 1 - core),
    }

    def block(c, p, half):
        return gathered.at[c, p // per_half, half, pl.ds((p % per_half) * r_piece, r_piece), :]

    def copy(c, p, way):
        return pltpu.make_async_remote_copy(
            src_ref=block(c, p, core), dst_ref=block(c, p, core),
            send_sem=send_sem.at[way, c, p], recv_sem=recv_sem.at[core, c, p],
            device_id=target[way], device_id_type=MESH,
        )

    def arrived(c, p, half):
        pltpu.make_async_remote_copy(
            src_ref=block(c, p, half), dst_ref=block(c, p, half),
            send_sem=send_sem.at[SIBLING, c, p], recv_sem=recv_sem.at[half, c, p],
            device_id=target[SIBLING], device_id_type=MESH,
        ).wait_recv()

    def x_copy(d, c):
        return pltpu.make_async_remote_copy(
            src_ref=send_buf.at[d - 1, c], dst_ref=recv_buf.at[d - 1, c],
            send_sem=x_send.at[d - 1, c], recv_sem=x_recv.at[d - 1, c],
            device_id={"width": lax.rem(wid + d, n_width)}, device_id_type=MESH,
        )

    w_copies = [
        pltpu.make_async_copy(
            weights.at[p // per_half, pl.ds((p % per_half) * r_piece, r_piece), :],
            block(chip, p, core), w_sem.at[p],
        )
        for p in range(pieces)
    ]
    for c in w_copies:
        c.start()
    tok_copy = pltpu.make_async_copy(tokens, tok, tok_sem)

    barrier = pltpu.get_barrier_semaphore()
    for way in range(4):
        pl.semaphore_signal(barrier, inc=1, device_id=target[way], device_id_type=MESH)
    for d in range(1, n_width):
        pl.semaphore_signal(
            barrier, inc=1, device_id={"width": lax.rem(wid + d, n_width)}, device_id_type=MESH
        )

    chunk = spread_mat.shape[0]
    wide = chunk * GROUP
    at_row = lax.broadcasted_iota(jnp.int32, (chunk, wide), 0)
    at_col = lax.broadcasted_iota(jnp.int32, (chunk, wide), 1)
    first_col = at_row * GROUP
    spread_mat[...] = jnp.where(
        (at_col >= first_col) & (at_col < first_col + GROUP), 1.0, 0.0
    ).astype(jnp.bfloat16)

    pl.semaphore_wait(barrier, 4 + n_width - 1)

    for p in range(pieces):
        g, row = p // per_half, (p % per_half) * r_piece
        w_copies[p].wait()

        @pl.loop(0, scales.shape[2] // chunk)
        def _(j):
            s = scales[g, pl.ds(row, r_piece), pl.ds(pl.multiple_of(j * chunk, chunk), chunk)]
            high = s.astype(jnp.bfloat16)
            rest = s - high.astype(jnp.float32)
            mid = rest.astype(jnp.bfloat16)
            low = (rest - mid.astype(jnp.float32)).astype(jnp.bfloat16)
            parts = jnp.dot(
                jnp.concatenate([high, mid, low], axis=0), spread_mat[...],
                preferred_element_type=jnp.float32,
            )
            spread = parts[:r_piece] + parts[r_piece:2 * r_piece] + parts[2 * r_piece:]
            cols = pl.ds(pl.multiple_of(j * wide, wide), wide)
            w = gathered[chip, g, core, pl.ds(row, r_piece), cols].astype(jnp.float32)
            gathered[chip, g, core, pl.ds(row, r_piece), cols] = (w * spread).astype(jnp.bfloat16)

        @pl.when(z > 0)
        def _():
            copy(chip, p, LEFT).start()

        @pl.when(z < n_z - 1)
        def _():
            copy(chip, p, RIGHT).start()

        copy(chip, p, ACROSS).start()
        copy(chip, p, SIBLING).start()
        if p == 0:
            tok_copy.start()

    tok_copy.wait()

    k_step = min(1024, depth)

    half_cols = n_cols // 2
    live = doc_lengths[0, 0]
    for k in range(1, doc_lengths.shape[1]):
        live = live + doc_lengths[0, k]
    position = wid * share + lax.broadcasted_iota(jnp.int32, (share, half_cols), 0)
    keep = position < live

    def multiply(load, slot):
        def rows_of(w):
            at_rows = pl.ds(pl.multiple_of(w * share, share), share)

            def dot(k):
                at = pl.ds(pl.multiple_of(k * k_step, k_step), k_step)
                return lax.dot_general(
                    tok[at_rows, at], load(at), (((1,), (1,)), ((), ())),
                    preferred_element_type=jnp.float32,
                )

            acc[...] = dot(0)

            @pl.loop(1, depth // k_step)
            def _(k):
                acc[...] += dot(k)

        for d in range(1, n_width):
            rows_of(lax.rem(wid + d, n_width))
            send_buf[d - 1, slot] = acc[...].astype(jnp.bfloat16)
            x_copy(d, slot).start()
        rows_of(wid)
        kept[slot] = acc[...]

    def total(slot):
        value = kept[slot]
        for d in range(1, n_width):
            x_copy(d, slot).wait_recv()
            value = value + recv_buf[d - 1, slot].astype(jnp.float32)
        return value

    def store(c, gate, up):
        mixed = jnp.where(keep, gate / (1.0 + jnp.exp(-gate)) * up, 0.0)
        if half_cols % 128 == 0:
            out[:, pl.ds(pl.multiple_of(c * half_cols, half_cols), half_cols)] = mixed
        else:
            for at in range(n_z * 2):
                @pl.when(c == at)
                def _():
                    out[:, at * half_cols:(at + 1) * half_cols] = mixed

    def compute(c):
        for p in range(pieces):
            arrived(c, p, 1 - core)
        multiply(lambda at: gathered[c, :, :, :, at].reshape(n_cols, k_step), c)

    def finish(c):
        value = total(c)
        store(c, value[:, :half_cols], value[:, half_cols:])

    def compute_pair(first, second, g):
        for p in range(g * per_half, (g + 1) * per_half):
            arrived(first, p, 1 - core)
            arrived(second, p, 1 - core)

        def load(at):
            return jnp.concatenate(
                [gathered[c, g, :, :, at].reshape(half_cols, k_step) for c in (first, second)],
                axis=0,
            )

        multiply(load, (first, second)[g])

    def finish_pair(first, second):
        gate, up = total(first), total(second)
        store(first, gate[:, :half_cols], up[:, :half_cols])
        store(second, gate[:, half_cols:], up[:, half_cols:])

    orders = []
    for zz in range(n_z):
        order = [zz]
        for r in range(1, n_z):
            order += [b for b in (zz - r, zz + r) if 0 <= b < n_z]
        orders.append(order)
    nearest = [pick([orders[zz][k] for zz in range(n_z)], z) for k in range(n_z)]
    half_way = n_z // 2
    lent = jnp.where(z < half_way, z + 1, z - 1)
    lend_left = (z > 0) & (z - 1 < half_way)
    lend_right = (z < n_z - 1) & (z + 1 >= half_way)
    lent_pieces = range(pieces // 2, pieces)

    def over_y(k, p):
        return nearest[k] != lent if p in lent_pieces and k > 0 else z >= 0

    def blocks_of(r):
        found = []
        if 0 < r < n_z:
            found.append((z - r >= 0, (z - r) * 2 + y))
            found.append((z + r < n_z, (z + r) * 2 + y))
        if r > 0:
            whole = nearest[r - 1] != lent if r > 1 else z >= 0
            found.append((whole, nearest[r - 1] * 2 + far))
        else:
            found.append((z >= 0, chip))
        return found

    def guarded(f, cond, c):
        @pl.when(cond)
        def _():
            f(c)

    lent_chip, last_chip = lent * 2 + far, nearest[n_z - 1] * 2 + far
    for r in range(1, n_z + 1):
        for p in range(pieces):
            if r < n_z:
                from_left, from_right = (z - r) * 2 + y, (z + r) * 2 + y

                @pl.when(z - r >= 0)
                def _():
                    arrived(from_left, p, core)

                    @pl.when(z < n_z - 1)
                    def _():
                        copy(from_left, p, RIGHT).start()

                    copy(from_left, p, SIBLING).start()

                @pl.when(z + r < n_z)
                def _():
                    arrived(from_right, p, core)

                    @pl.when(z > 0)
                    def _():
                        copy(from_right, p, LEFT).start()

                    copy(from_right, p, SIBLING).start()

                @pl.when(over_y(r, p))
                def _():
                    copy(nearest[r] * 2 + y, p, ACROSS).start()

            @pl.when(over_y(r - 1, p))
            def _():
                c = nearest[r - 1] * 2 + far
                arrived(c, p, core)
                copy(c, p, SIBLING).start()

            if r == n_z and p in lent_pieces:
                arrived(lent_chip, p, core)
                copy(lent_chip, p, SIBLING).start()

            ready = blocks_of(r - 1)
            if r == n_z:
                if p == 0:
                    for cond, c in ready[:2]:
                        guarded(compute, cond, c)
                elif p == per_half - 1:
                    for cond, c in ready[2:]:
                        guarded(compute, cond, c)
                elif p == pieces * 5 // 8:
                    compute_pair(last_chip, lent_chip, 0)
                    for old in (r - 2, r - 1):
                        for cond, c in blocks_of(old):
                            guarded(finish, cond, c)
            elif p < len(ready):
                guarded(compute, *ready[p])
            if 1 < r < n_z and p == pieces - 1:
                for cond, c in blocks_of(r - 2):
                    guarded(finish, cond, c)

        if r == n_z - 1:
            own_far = z * 2 + far
            for p in lent_pieces:
                @pl.when(lend_left)
                def _():
                    copy(own_far, p, LEFT).start()

                @pl.when(lend_right)
                def _():
                    copy(own_far, p, RIGHT).start()

    compute_pair(last_chip, lent_chip, 1)
    finish_pair(last_chip, lent_chip)

    for zz in range(n_z):
        for p in range(pieces):
            own, other = zz * 2 + y, zz * 2 + far

            @pl.when((z > 0) & (z <= zz))
            def _():
                copy(own, p, LEFT).wait_send()

            @pl.when((z < n_z - 1) & (z >= zz))
            def _():
                copy(own, p, RIGHT).wait_send()

            if p in lent_pieces:
                @pl.when((zz == z) & lend_left)
                def _():
                    copy(other, p, LEFT).wait_send()

                @pl.when((zz == z) & lend_right)
                def _():
                    copy(other, p, RIGHT).wait_send()

                @pl.when(zz != lent)
                def _():
                    copy(own, p, ACROSS).wait_send()
            else:
                copy(own, p, ACROSS).wait_send()
            copy(own, p, SIBLING).wait_send()
            copy(other, p, SIBLING).wait_send()
    for c in range(n_z * 2):
        for d in range(1, n_width):
            x_copy(d, c).wait_send()


def per_device(tokens, panel_weights, panel_scales, doc_lengths):
    n_seq, n_width = lax.axis_size("seq"), lax.axis_size("width")
    n_tok, depth = tokens.shape
    cols = panel_weights.shape[2]
    share = n_tok // n_width
    chips = n_seq // 2
    pieces = 4
    chunk = min(128, panel_scales.shape[1])
    bf16, f32 = jnp.bfloat16, jnp.float32
    return pl.pallas_call(
        functools.partial(kernel, n_seq, n_width, pieces),
        out_shape=jax.ShapeDtypeStruct((share, cols * n_seq), f32),
        in_specs=[
            pl.BlockSpec(memory_space=pl.ANY),
            pl.BlockSpec(memory_space=pltpu.VMEM),
            pl.BlockSpec(memory_space=pl.ANY),
            pl.BlockSpec(memory_space=pltpu.SMEM),
        ],
        out_specs=pl.BlockSpec(memory_space=pltpu.VMEM),
        scratch_shapes=[
            pltpu.VMEM((chips, 2, 2, cols, depth), bf16),
            pltpu.VMEM((n_tok, depth), bf16),
            pltpu.VMEM((chunk, chunk * GROUP), bf16),
            pltpu.VMEM((share, 4 * cols), f32),
            pltpu.VMEM((chips, share, 4 * cols), f32),
            pltpu.VMEM((max(n_width - 1, 1), chips, share, 4 * cols), bf16),
            pltpu.VMEM((max(n_width - 1, 1), chips, share, 4 * cols), bf16),
            pltpu.SemaphoreType.DMA((4, chips, pieces)),
            pltpu.SemaphoreType.DMA((2, chips, pieces)),
            pltpu.SemaphoreType.DMA((max(n_width - 1, 1), chips)),
            pltpu.SemaphoreType.DMA((max(n_width - 1, 1), chips)),
            pltpu.SemaphoreType.DMA((pieces,)),
            pltpu.SemaphoreType.DMA,
        ],
        compiler_params=pltpu.CompilerParams(
            collective_id=0, has_side_effects=True, vmem_limit_bytes=62 * 1024 * 1024
        ),
        cost_estimate=pl.CostEstimate(
            flops=2 * n_tok * depth * 2 * cols * n_seq,
            bytes_accessed=2 * n_tok * depth + 4 * cols * depth,
            transcendentals=share * cols * n_seq,
        ),
    )(jnp.swapaxes(panel_weights, 1, 2), jnp.swapaxes(panel_scales, 1, 2), tokens, doc_lengths)


def solution(mesh):
    in_specs = (P("seq", "width"), P(None, "width", "seq"), P(None, "width", "seq"), P("seq", None))
    out_specs = P(("seq", "width"), None)
    return jax.shard_map(
        per_device, mesh=mesh, in_specs=in_specs, out_specs=out_specs, check_vma=False
    )
```
